32 devices in a mesh: groups: 2 (over y), dom: 4 (over z), mp: 4 (over x, core).
Axes of the slice: x: 2, y: 2, z: 4, core: 2. Of those that a mesh axis runs over, the one named last changes fastest.
Arguments:
- nodes: float32 [1536, 512], P(('groups', 'dom', 'mp')), parts along dimension 0, may hold values from -6 to 6
- edges: float32 [12288, 512], P(('groups', 'dom', 'mp')), parts along dimension 0, may hold values from -6 to 6
- senders: int32 [6144], P(('dom', 'mp')), may hold values from 0 to 71
- receivers: int32 [6144], P(('dom', 'mp')), may hold values from 0 to 48, as said below
- halo_rows: int32 [384], P(('dom', 'mp')), may hold values from 0 to 47
- drop_mask: int32 [6144], P(('dom', 'mp')), may hold values 0 or 1
- w_in: float32 [1536, 512], P('mp'), may hold values from -0.15625 to 0.15625
- w_out: float32 [512, 512], P('mp'), may hold values from -0.25 to 0.25
- cotangent: float32 [12288, 512], P(('groups', 'dom', 'mp')), parts along dimension 0, may hold values from -6 to 6
Outputs:
- grad_nodes: float32 [1536, 512], P(('groups', 'dom', 'mp')), parts along dimension 0
- grad_edges: float32 [12288, 512], P(('groups', 'dom', 'mp')), parts along dimension 0
- grad_w_in: float32 [3072, 512], P(('groups', 'mp')), parts along dimension 0
- grad_w_out: float32 [1024, 512], P(('groups', 'mp')), parts along dimension 0
The draws below stay inside these ranges and needn't reach their ends.
There are 2 independent parts, one for each index of `groups`. The reference program is written for one: setup_inputs(seed, part) draws one part's arguments, and reference() takes and returns one part's arrays. A program takes and returns all parts, laid end to end along the dimension named above; an argument that names none is the same for every part. Nothing has to cross between parts.
Inputs may be any that keep to these rules, and one draw needn't show every extreme that they name: `receivers`: each partition's 384 ids are non-decreasing and start at 0; ids below 48 name a node of that partition, 48 marks padding, and every partition has some padding at its end and real edges in at least half of its slots.
All inputs are finite; a program needn't handle non-finite values. No bound on the sum of `drop_mask` on one device may be relied on, other than what follows from the above.
Results may differ from the reference program's by a relative error of at most 0.00012.
Values sent between devices are 32-bit elements; how exact they have to be, the bound alone decides.
A program may use at most 64 MiB of HBM per device.

```python
import math
import jax
import jax.numpy as jnp
from jax import lax

D = 512
M_DEV = 48
E_DEV = 384
HALO = 12
NODES = 768
EDGES = 6144
HALO_ROWS = 384
N_DOM = 4
N_MP = 4


def draw_receivers(key, part):
    key = jax.random.fold_in(key, 7)
    count_key, value_key = jax.random.split(key)
    blocks = EDGES // E_DEV
    values = jnp.sort(jax.random.randint(value_key, (blocks, E_DEV), 0, M_DEV), axis=1)
    position = jnp.arange(E_DEV, dtype=jnp.int32)[None, :]
    values = jnp.where(position == 0, 0, values)
    filled = E_DEV - 1 - jax.random.randint(count_key, (blocks, 1), 0, E_DEV // 2)
    return jnp.where(position < filled, values, M_DEV).astype(jnp.int32).reshape(EDGES)


def place_ends(entries, stream_key, least, largest):
    longest = entries.shape.index(max(entries.shape))
    spots = []
    for shift in (0, 1):
        where = [jax.random.randint(jax.random.fold_in(stream_key, axis), (), 0, length) for axis, length in enumerate(entries.shape)]
        where[longest] = (where[longest] + shift) % entries.shape[longest]
        spots.append(tuple(where))
    return entries.at[spots[0]].set(least).at[spots[1]].set(largest)


def block_levels(rng, shape, cuts, least, high):
    def one(dim, blocks):
        steps = jax.random.uniform(jax.random.fold_in(jax.random.fold_in(rng, 6), dim), (blocks,), jnp.float32, least / len(cuts), high / len(cuts))
        return jnp.repeat(jnp.exp(steps), shape[dim] // blocks).reshape((-1,) + (1,) * (len(shape) - dim - 1))

    level = one(*cuts[0])
    for cut in cuts[1:]:
        level = level * one(*cut)
    return level


def gaussian(stream_key, shape, deviation, limit, cuts=(), held_as=jnp.bfloat16):
    entries = deviation * jax.random.normal(stream_key, shape, jnp.float32)
    if cuts:
        entries = entries * block_levels(stream_key, shape, cuts, -0.22, 0.18)
    return jnp.clip(entries, -limit, limit).astype(held_as)


def setup_inputs(seed: int = 0, part: int = 0) -> dict:
    keys = jax.random.split(jax.random.key(seed), 10)
    part_splits = jax.random.split(jax.random.fold_in(keys[9], part), 10)
    return {
        "nodes": gaussian(part_splits[0], (NODES, D), 1.0, 6.0, ((0, 16),), jnp.float32),
        "edges": gaussian(part_splits[1], (EDGES, D), 1.0, 6.0, ((0, 16),), jnp.float32),
        "senders": place_ends(jax.random.randint(keys[2], (EDGES,), 0, M_DEV + 2 * HALO), jax.random.fold_in(keys[2], 1), 0, (M_DEV + 2 * HALO) - 1).astype(jnp.int32),
        "receivers": draw_receivers(jax.random.fold_in(keys[9], 71), part),
        "halo_rows": place_ends(jax.random.randint(keys[4], (HALO_ROWS,), 0, M_DEV), jax.random.fold_in(keys[4], 1), 0, M_DEV - 1).astype(jnp.int32),
        "drop_mask": place_ends((jax.random.randint(keys[5], (EDGES,), 0, 10) < 9).astype(jnp.int32), jax.random.fold_in(keys[5], 1), 0, 1),
        "w_in": gaussian(keys[6], (3 * D, D), (3 * D) ** -0.5, 0.15625, ((0, 4),), jnp.float32),
        "w_out": gaussian(keys[7], (D, D), D ** -0.5, 0.25, ((0, 4),), jnp.float32),
        "cotangent": gaussian(part_splits[8], (EDGES, D), 1.0, 6.0, ((0, 16),), jnp.float32),
    }


def forward(nodes, edges, w_in, w_out, source, target, keep):
    joined = jnp.concatenate([edges, nodes[source], nodes[target]], axis=1)
    hidden_in = jnp.dot(joined, w_in, preferred_element_type=jnp.float32, precision=lax.Precision.HIGHEST)
    hidden = hidden_in * jax.nn.sigmoid(hidden_in)
    message = jnp.dot(hidden, w_out, preferred_element_type=jnp.float32, precision=lax.Precision.HIGHEST)
    centre = lax.optimization_barrier(jnp.mean(message, axis=1, keepdims=True))
    variance = lax.optimization_barrier(jnp.mean(message * message, axis=1, keepdims=True)) - centre * centre
    normed = (message - centre) * lax.rsqrt(variance + 1e-05)
    return edges + keep * normed

def reference(nodes, edges, senders, receivers, halo_rows, drop_mask, w_in, w_out, cotangent):
    count = N_DOM * N_MP
    owner = (jnp.arange(EDGES, dtype=jnp.int32) // E_DEV).astype(jnp.int32)
    before = ((owner - 1) % count).astype(jnp.int32)
    after = ((owner + 1) % count).astype(jnp.int32)
    from_before = halo_rows[(before * (2 * HALO) + jnp.clip(senders - M_DEV, 0, HALO - 1)).astype(jnp.int32)]
    from_after = halo_rows[(after * (2 * HALO) + HALO + jnp.clip(senders - M_DEV - HALO, 0, HALO - 1)).astype(jnp.int32)]
    source = jnp.where(senders < M_DEV, owner * M_DEV + jnp.minimum(senders, M_DEV - 1), jnp.where(senders < M_DEV + HALO, before * M_DEV + from_before, after * M_DEV + from_after)).astype(jnp.int32)
    target = (owner * M_DEV + jnp.minimum(receivers, M_DEV - 1)).astype(jnp.int32)
    keep = jnp.where((receivers < M_DEV) & (drop_mask == 1), jnp.float32(1.0 / 0.9), jnp.float32(0.0))[:, None]

    def apply_layer(node_in, edge_in, first, second):
        return forward(node_in, edge_in, first, second, source, target, keep)
    updated, pullback = jax.vjp(apply_layer, nodes, edges, w_in, w_out)
    grad_nodes, grad_edges, grad_first, grad_second = pullback(cotangent)
    factor = 1.0 / math.sqrt(EDGES)
    return (grad_nodes, grad_edges, grad_first * factor, grad_second * factor)
```

```python
import functools
import math

import jax
import jax.numpy as jnp
from jax import lax
from jax.experimental import pallas as pl
from jax.experimental.pallas import tpu as pltpu
from jax.sharding import PartitionSpec as P

norm_epsilon = 1e-05
keep_scale = 1.0 / 0.9
MESH = pl.DeviceIdType.MESH
f32, bf16 = jnp.float32, jnp.bfloat16


def split(value):
    high = value.astype(bf16)
    return high, (value - high.astype(f32)).astype(bf16)


def product(left, right, contract):
    return lax.dot_general(left, right, ((contract[:1], contract[1:]), ((), ())), preferred_element_type=f32)


def product3(left, right, contract):
    (lh, ll), (rh, rl) = left, right
    return product(lh, rh, contract) + (product(lh, rl, contract) + product(ll, rh, contract))


def product2(exact, right, contract):
    rh, rl = right
    return product(exact, rh, contract) + product(exact, rl, contract)


def pick(pair, rows):
    return pair[0][rows], pair[1][rows]


def kernel(
    sizes,
    nodes_ref, edges_ref, senders_ref, receivers_ref, halo_ref, drop_ref, win_ref, wout_ref, cot_ref,
    gnodes_ref, gedges_ref, gwin_ref, gwout_ref,
    table, full_in, full_out, halo_send, back_send, back_recv, gin, gout,
    from_core, x_send, from_x, acc, from_outer, from_inner, total,
    gather_send, gather_recv, halo_ssem, halo_rsem, core_ssem, core_rsem, x_ssem, x_rsem,
    outer_rsem, inner_rsem, inward_ssem, outward_ssem,
):
    groups, doms, chunk = sizes["groups"], sizes["dom"], sizes["chunk"]
    count_parts = doms * 4
    g, d, m = lax.axis_index("groups"), lax.axis_index("dom"), lax.axis_index("mp")
    x, c = m // 2, m % 2
    far = 1 - x
    part = d * 4 + m
    after, before = (part + 1) % count_parts, (part + count_parts - 1) % count_parts
    core_peer = (g, d, 2 * x + (1 - c))
    x_peer = (g, d, 2 * far + c)
    y_peer = (1 - g, d, m)
    next_peer = (g, after // 4, after % 4)
    prev_peer = (g, before // 4, before % 4)
    left_half = d < doms // 2
    inner = jnp.where(left_half, d + 1, d - 1)
    outer = jnp.where(left_half, d - 1, d + 1)
    has_outer = (d > 0) & (d < doms - 1)
    is_mid = (d == doms // 2 - 1) | (d == doms // 2)
    inner_peer, outer_peer = (g, inner, m), (g, outer, m)
    helped = groups == 2

    barrier = pltpu.get_barrier_semaphore()
    partners = [core_peer, x_peer, next_peer, prev_peer, inner_peer] + ([y_peer] if helped else [])
    for peer in partners:
        pl.semaphore_signal(barrier, inc=1, device_id=peer, device_id_type=MESH)

    @pl.when(has_outer)
    def _():
        pl.semaphore_signal(barrier, inc=1, device_id=outer_peer, device_id_type=MESH)
        pl.semaphore_wait(barrier, len(partners) + 1)

    @pl.when(jnp.logical_not(has_outer))
    def _():
        pl.semaphore_wait(barrier, len(partners))

    def remote(src, dst, send, recv, peer):
        return pltpu.make_async_remote_copy(
            src_ref=src, dst_ref=dst, send_sem=send, recv_sem=recv, device_id=peer, device_id_type=MESH
        )

    rows_in, rows_out = win_ref.shape[0], wout_ref.shape[0]
    depth = full_out.shape[0]
    count_nodes, count_edges = nodes_ref.shape[0], edges_ref.shape[0]
    padded = halo_send.shape[1]
    parts = 2 if helped else 1
    mine, other = (g, 1 - g) if helped else (0, 0)
    half_in, half_out = rows_in // parts, rows_out // parts
    pieces = [(0, 0, half_in // 2), (0, half_in // 2, half_in // 2), (1, 0, half_out)]

    def rows_at(start, size):
        return pl.ds(pl.multiple_of(start, 8), size)

    def piece_of(owner, which, number):
        kind, offset, size = pieces[number]
        if kind == 0:
            return full_in.at[rows_at(owner * rows_in + which * half_in + offset, size)]
        return full_out.at[rows_at(owner * rows_out + which * half_out + offset, size)]

    def own_piece(which, number):
        kind, offset, size = pieces[number]
        if kind == 0:
            return win_ref.at[rows_at(which * half_in + offset, size)]
        return wout_ref.at[rows_at(which * half_out + offset, size)]

    x_copies, y_copies, fx_copies, fy_copies = [], [], [], []
    for number in range(3):
        copy = remote(own_piece(mine, number), piece_of(m, mine, number), gather_send.at[1, number], gather_recv.at[1, number], x_peer)
        copy.start()
        x_copies.append(copy)
    whole_in = remote(win_ref, full_in.at[rows_at(m * rows_in, rows_in)], gather_send.at[0, 0], gather_recv.at[0, 0], core_peer)
    whole_out = remote(wout_ref, full_out.at[rows_at(m * rows_out, rows_out)], gather_send.at[0, 1], gather_recv.at[0, 1], core_peer)
    whole_in.start()
    whole_out.start()

    halo_hit = lax.broadcasted_iota(jnp.int32, (count_nodes, 128), 0) == halo_ref[...]
    halo_hot = jnp.where(halo_hit, 1.0, 0.0)
    halo_pick = jnp.transpose(halo_hot)[: 2 * padded].astype(bf16)
    halo_hot = halo_hot.astype(bf16)[:, : 2 * padded]
    nodes = nodes_ref[...]
    nh, nl = split(nodes)
    nr = (nodes - nh.astype(f32) - nl.astype(f32)).astype(bf16)
    listed = product(halo_pick, nh, (1, 0)) + (product(halo_pick, nl, (1, 0)) + product(halo_pick, nr, (1, 0)))
    halo_send[0] = listed[:padded]
    halo_send[1] = listed[padded:]
    first_at, last_at = pl.ds(count_nodes, padded), pl.ds(count_nodes + padded, padded)
    to_next = remote(halo_send.at[0], table.at[first_at], halo_ssem.at[0], halo_rsem.at[0], next_peer)
    to_prev = remote(halo_send.at[1], table.at[last_at], halo_ssem.at[1], halo_rsem.at[1], prev_peer)
    to_next.start()
    to_prev.start()
    slots = count_nodes + 2 * padded
    table[0:count_nodes] = nodes
    table[slots : slots + count_nodes] = nodes

    halo_size = sizes["halo"]
    senders = senders_ref[...]
    senders = jnp.where(senders < count_nodes + halo_size, senders, senders + (padded - halo_size))
    receivers = receivers_ref[...]
    targets = slots + jnp.minimum(receivers, count_nodes - 1)
    total_slots = slots + count_nodes
    index = lax.broadcasted_iota(jnp.int32, (total_slots, count_edges), 0)
    hot = jnp.where((index == senders) | (index == targets), 1.0, 0.0)
    hot_t = hot.astype(bf16)
    hot = jnp.transpose(hot).astype(bf16)
    keep = jnp.where((receivers < count_nodes) & (drop_ref[...] == 1), f32(keep_scale), f32(0.0))
    keep = jnp.transpose(jnp.broadcast_to(keep, (128, count_edges)))[:, :1]

    full_in[rows_at(m * rows_in, rows_in)] = win_ref[...]
    full_out[rows_at(m * rows_out, rows_out)] = wout_ref[...]
    edges = split(edges_ref[...])

    peer_x, peer_core, peer_far = 2 * far + c, 2 * x + (1 - c), 2 * far + (1 - c)

    def forward_x(number):
        x_copies[number].wait_recv()
        block = piece_of(peer_x, mine, number)
        copy = remote(block, block, gather_send.at[3, number], gather_recv.at[3, number], core_peer)
        if helped:
            along = remote(block, block, gather_send.at[2, number], gather_recv.at[2, number], y_peer)
            along.start()
            y_copies.append(along)
        copy.start()
        fx_copies.append(copy)

    def forward_y(number):
        if helped:
            y_copies[number].wait_recv()
            block = piece_of(peer_x, other, number)
            copy = remote(block, block, gather_send.at[4, number], gather_recv.at[4, number], core_peer)
            copy.start()
            fy_copies.append(copy)

    forward_x(0)
    forward_x(1)
    forward_y(0)
    forward_x(2)
    forward_y(1)
    whole_in.wait_recv()
    to_next.wait_recv()
    to_prev.wait_recv()
    for number in range(2):
        fx_copies[number].wait_recv()
        if helped:
            fy_copies[number].wait_recv()

    w_a = split(full_in[0:depth])
    w_b = split(full_in[depth : 2 * depth])
    w_c = split(full_in[2 * depth : 3 * depth])
    table_pair = split(table[...])
    ends = jnp.concatenate(
        [
            product3(pick(table_pair, slice(0, slots)), w_b, (1, 0)),
            product3(pick(table_pair, slice(slots, total_slots)), w_c, (1, 0)),
        ],
        axis=0,
    )
    hidden_in = product3(edges, w_a, (1, 0)) + product2(hot, split(ends), (1, 0))
    gate = jax.nn.sigmoid(hidden_in)
    hidden = split(hidden_in * gate)
    slope = gate + hidden_in * gate * (1.0 - gate)

    forward_y(2)
    whole_out.wait_recv()
    fx_copies[2].wait_recv()
    if helped:
        fy_copies[2].wait_recv()
    w_o = split(full_out[...])
    message = product3(hidden, w_o, (1, 0))
    centre = jnp.mean(message, axis=1, keepdims=True)
    variance = jnp.mean(message * message, axis=1, keepdims=True) - centre * centre
    scale = lax.rsqrt(variance + norm_epsilon)
    normed = (message - centre) * scale
    weighted = keep * cot_ref[...]
    grad_message = split(
        scale
        * (
            weighted
            - jnp.mean(weighted, axis=1, keepdims=True)
            - normed * jnp.mean(weighted * normed, axis=1, keepdims=True)
        )
    )
    gout[...] = product3(hidden, grad_message, (0, 0))

    blocks = [(1, start) for start in range(0, rows_out, chunk)] + [(0, start) for start in range(0, rows_in, chunk)]
    first_in = rows_out // chunk

    def grad_rows(owner, number):
        kind, start = blocks[number]
        if kind == 1:
            return gout.at[rows_at(owner * rows_out + start, chunk)]
        return gin.at[rows_at(owner * rows_in + start, chunk)]

    core_copies, x_grad_copies = {}, {}

    def swap_cores(numbers):
        for side, owner in ((0, peer_far), (1, peer_core)):
            for number in numbers:
                copy = remote(
                    grad_rows(owner, number), from_core.at[side, number],
                    core_ssem.at[side, number], core_rsem.at[side, number], core_peer,
                )
                copy.start()
                core_copies[side, number] = copy

    def swap_x(numbers):
        for number in numbers:
            core_copies[0, number].wait_recv()
            x_send[number] = grad_rows(peer_x, number)[...] + from_core[0, number]
            copy = remote(x_send.at[number], from_x.at[number], x_ssem.at[number], x_rsem.at[number], x_peer)
            copy.start()
            x_grad_copies[number] = copy

    early, late = range(first_in), range(first_in, len(blocks))
    swap_cores(early)
    grad_hidden = split(product3(grad_message, w_o, (1, 1)) * slope)
    swap_x(early)
    sums = product2(hot_t, grad_hidden, (1, 0))
    slot = lax.broadcasted_iota(jnp.int32, sums.shape, 0)
    gin[depth : 2 * depth] = product3(table_pair, split(jnp.where(slot < slots, sums, 0.0)), (0, 0))
    gin[2 * depth : 3 * depth] = product3(table_pair, split(jnp.where(slot < slots, 0.0, sums)), (0, 0))
    gin[0:depth] = product3(edges, grad_hidden, (0, 0))
    swap_cores(late)

    sums = split(sums)
    grad_table = product3(pick(sums, slice(0, slots)), w_b, (1, 1))
    back_send[0] = grad_table[count_nodes : count_nodes + padded]
    back_send[1] = grad_table[count_nodes + padded : slots]
    back_prev = remote(back_send.at[0], back_recv.at[pl.ds(0, padded)], halo_ssem.at[2], halo_rsem.at[2], prev_peer)
    back_next = remote(back_send.at[1], back_recv.at[pl.ds(padded, padded)], halo_ssem.at[3], halo_rsem.at[3], next_peer)
    back_prev.start()
    back_next.start()
    swap_x(late)
    own = grad_table[:count_nodes] + product3(pick(sums, slice(slots, total_slots)), w_c, (1, 1))
    gedges_ref[...] = cot_ref[...] + product3(grad_hidden, w_a, (1, 1))
    back_prev.wait_recv()
    back_next.wait_recv()
    gnodes_ref[...] = own + product2(halo_hot, split(back_recv[...]), (1, 0))

    def inward(number, to_mid):
        landing = (from_inner, inner_rsem) if to_mid else (from_outer, outer_rsem)
        return remote(acc.at[number], landing[0].at[number], inward_ssem.at[number], landing[1].at[number], inner_peer)

    def outward(number):
        return remote(total.at[number], from_inner.at[number], outward_ssem.at[number], inner_rsem.at[number], outer_peer)

    def collect(number):
        core_copies[1, number].wait_recv()
        x_grad_copies[number].wait_recv()
        acc[number] = grad_rows(m, number)[...] + from_core[1, number] + from_x[number]

        @pl.when(has_outer)
        def _():
            inward(number, False).wait_recv()
            acc[number] = acc[number] + from_outer[number]

        @pl.when(is_mid)
        def _():
            inward(number, True).start()

        @pl.when(jnp.logical_not(is_mid))
        def _():
            inward(number, False).start()

    factor = f32(sizes["factor"])

    def finish(number, sends):
        kind, start = blocks[number]
        inward(number, True).wait_recv()

        @pl.when(is_mid)
        def _():
            total[number] = acc[number] + from_inner[number]

        @pl.when(jnp.logical_not(is_mid))
        def _():
            total[number] = from_inner[number]

        if sends:
            outward(number).start()
        result = gwout_ref if kind == 1 else gwin_ref
        result[pl.ds(start, chunk)] = total[number] * factor

    lag = 2
    for number in range(len(blocks) + lag):
        if number < len(blocks):
            collect(number)
        if number >= lag:

            @pl.when(has_outer)
            def _():
                finish(number - lag, True)

    @pl.when(jnp.logical_not(has_outer))
    def _():
        for number in range(len(blocks)):
            finish(number, False)

    for copy in [whole_in, whole_out, to_next, to_prev, back_prev, back_next] + x_copies + y_copies + fx_copies + fy_copies:
        copy.wait_send()
    for number in range(len(blocks)):
        core_copies[0, number].wait_send()
        core_copies[1, number].wait_send()
        x_grad_copies[number].wait_send()
        inward(number, True).wait_send()

    @pl.when(has_outer)
    def _():
        for number in range(len(blocks)):
            outward(number).wait_send()


def body(mesh_shape, nodes, edges, senders, receivers, halo_rows, drop_mask, w_in, w_out, cotangent):
    count_nodes, depth = nodes.shape
    count_edges = edges.shape[0]
    halo_size = halo_rows.shape[0] // 2
    padded = -(-halo_size // 16) * 16
    doms = mesh_shape["dom"]
    chunk = math.gcd(w_in.shape[0], w_out.shape[0]) // 2
    count = (w_in.shape[0] + w_out.shape[0]) // chunk
    sizes = {
        "groups": mesh_shape["groups"],
        "dom": doms,
        "chunk": chunk,
        "halo": halo_size,
        "factor": 1.0 / math.sqrt(count_edges * doms * mesh_shape["mp"]),
    }
    gap = jnp.full((padded - halo_size,), -1, jnp.int32)
    rest = jnp.full((128 - 2 * padded,), -1, jnp.int32)
    halo = jnp.concatenate([halo_rows[:halo_size], gap, halo_rows[halo_size:], gap, rest])[None, :]
    vmem = pl.BlockSpec(memory_space=pltpu.VMEM)
    piece = (count, chunk, depth)
    dma = pltpu.SemaphoreType.DMA
    return pl.pallas_call(
        functools.partial(kernel, sizes),
        out_shape=(
            jax.ShapeDtypeStruct(nodes.shape, f32),
            jax.ShapeDtypeStruct(edges.shape, f32),
            jax.ShapeDtypeStruct(w_in.shape, f32),
            jax.ShapeDtypeStruct(w_out.shape, f32),
        ),
        in_specs=[vmem] * 9,
        out_specs=(vmem,) * 4,
        scratch_shapes=[
            pltpu.VMEM((2 * count_nodes + 2 * padded, depth), f32),
            pltpu.VMEM((3 * depth, depth), f32),
            pltpu.VMEM((depth, depth), f32),
            pltpu.VMEM((2, padded, depth), f32),
            pltpu.VMEM((2, padded, depth), f32),
            pltpu.VMEM((2 * padded, depth), f32),
            pltpu.VMEM((3 * depth, depth), f32),
            pltpu.VMEM((depth, depth), f32),
            pltpu.VMEM((2,) + piece, f32),
            pltpu.VMEM(piece, f32),
            pltpu.VMEM(piece, f32),
            pltpu.VMEM(piece, f32),
            pltpu.VMEM(piece, f32),
            pltpu.VMEM(piece, f32),
            pltpu.VMEM(piece, f32),
            dma((5, 3)),
            dma((5, 3)),
            dma((4,)),
            dma((4,)),
            dma((2, count)),
            dma((2, count)),
            dma((count,)),
            dma((count,)),
            dma((count,)),
            dma((count,)),
            dma((count,)),
            dma((count,)),
        ],
        compiler_params=pltpu.CompilerParams(
            collective_id=0, has_side_effects=True, vmem_limit_bytes=56 * 1024 * 1024
        ),
    )(
        nodes, edges, senders[None, :], receivers[None, :], halo, drop_mask[None, :], w_in, w_out, cotangent
    )


def solution(mesh):
    return jax.shard_map(
        functools.partial(body, dict(mesh.shape)),
        mesh=mesh,
        in_specs=(
            P(("groups", "dom", "mp"), None),
            P(("groups", "dom", "mp"), None),
            P(("dom", "mp")),
            P(("dom", "mp")),
            P(("dom", "mp")),
            P(("dom", "mp")),
            P("mp", None),
            P("mp", None),
            P(("groups", "dom", "mp"), None),
        ),
        out_specs=(
            P(("groups", "dom", "mp"), None),
            P(("groups", "dom", "mp"), None),
            P(("groups", "mp"), None),
            P(("groups", "mp"), None),
        ),
        check_vma=False,
    )
```

```python
import functools
import math

import jax
import jax.numpy as jnp
from jax import lax
from jax.experimental import pallas as pl
from jax.experimental.pallas import tpu as pltpu
from jax.sharding import PartitionSpec as P

norm_epsilon = 1e-05
keep_scale = 1.0 / 0.9
MESH = pl.DeviceIdType.MESH
f32, bf16 = jnp.float32, jnp.bfloat16


def split(value):
    high = value.astype(bf16)
    return high, (value - high.astype(f32)).astype(bf16)


def product(left, right, contract):
    return lax.dot_general(left, right, ((contract[:1], contract[1:]), ((), ())), preferred_element_type=f32)


def product3(left, right, contract):
    (lh, ll), (rh, rl) = left, right
    return product(lh, rh, contract) + (product(lh, rl, contract) + product(ll, rh, contract))


def product2(exact, right, contract):
    rh, rl = right
    return product(exact, rh, contract) + product(exact, rl, contract)


def pick(pair, rows):
    return pair[0][rows], pair[1][rows]


def kernel(
    sizes,
    nodes_ref, edges_ref, senders_ref, receivers_ref, halo_ref, drop_ref, win_ref, wout_ref, cot_ref,
    gnodes_ref, gedges_ref, gwin_ref, gwout_ref,
    table, full_in, full_out, halo_send, back_send, back_recv, gin, gout,
    from_core, x_send, from_x, acc, from_outer, from_inner, total,
    gather_send, gather_recv, halo_ssem, halo_rsem, core_ssem, core_rsem, x_ssem, x_rsem,
    outer_rsem, inner_rsem, inward_ssem, outward_ssem,
    edges_in, cot, grad_edges, own, local_sem,
):
    groups, doms = sizes["groups"], sizes["dom"]
    count_parts = doms * 4
    g, d, m = lax.axis_index("groups"), lax.axis_index("dom"), lax.axis_index("mp")
    x, c = m // 2, m % 2
    far = 1 - x
    part = d * 4 + m
    after, before = (part + 1) % count_parts, (part + count_parts - 1) % count_parts
    core_peer = (g, d, 2 * x + (1 - c))
    x_peer = (g, d, 2 * far + c)
    y_peer = (1 - g, d, m)
    next_peer = (g, after // 4, after % 4)
    prev_peer = (g, before // 4, before % 4)
    left_half = d < doms // 2
    inner = jnp.where(left_half, d + 1, d - 1)
    outer = jnp.where(left_half, d - 1, d + 1)
    has_outer = (d > 0) & (d < doms - 1)
    is_mid = (d == doms // 2 - 1) | (d == doms // 2)
    inner_peer, outer_peer = (g, inner, m), (g, outer, m)
    helped = groups == 2

    loads = [
        pltpu.make_async_copy(edges_ref, edges_in, local_sem.at[0]),
        pltpu.make_async_copy(cot_ref, cot, local_sem.at[1]),
        pltpu.make_async_copy(win_ref, full_in.at[pl.ds(pl.multiple_of(m * win_ref.shape[0], 8), win_ref.shape[0])], local_sem.at[2]),
        pltpu.make_async_copy(wout_ref, full_out.at[pl.ds(pl.multiple_of(m * wout_ref.shape[0], 8), wout_ref.shape[0])], local_sem.at[3]),
    ]
    barrier = pltpu.get_barrier_semaphore()
    partners = [core_peer, x_peer, next_peer, prev_peer, inner_peer] + ([y_peer] if helped else [])
    for peer in partners:
        pl.semaphore_signal(barrier, inc=1, device_id=peer, device_id_type=MESH)

    @pl.when(has_outer)
    def _():
        pl.semaphore_signal(barrier, inc=1, device_id=outer_peer, device_id_type=MESH)
        pl.semaphore_wait(barrier, len(partners) + 1)

    @pl.when(jnp.logical_not(has_outer))
    def _():
        pl.semaphore_wait(barrier, len(partners))

    for load in loads:
        load.start()

    def remote(src, dst, send, recv, peer):
        return pltpu.make_async_remote_copy(
            src_ref=src, dst_ref=dst, send_sem=send, recv_sem=recv, device_id=peer, device_id_type=MESH
        )

    rows_in, rows_out = win_ref.shape[0], wout_ref.shape[0]
    depth = full_out.shape[0]
    count_nodes, count_edges = nodes_ref.shape[0], edges_ref.shape[0]
    padded = halo_send.shape[1]
    parts = 2 if helped else 1
    mine, other = (g, 1 - g) if helped else (0, 0)
    half_in, half_out = rows_in // parts, rows_out // parts
    pieces, start = [], 0
    for share in sizes["gather_in"]:
        pieces.append((0, start, half_in * share // sum(sizes["gather_in"])))
        start += pieces[-1][2]
    count_in, start = len(pieces), 0
    for share in sizes["gather_out"]:
        pieces.append((1, start, half_out * share // sum(sizes["gather_out"])))
        start += pieces[-1][2]
    last = len(pieces)

    def rows_at(start, size):
        return pl.ds(pl.multiple_of(start, 8), size)

    def piece_of(owner, which, number):
        kind, offset, size = pieces[number]
        if kind == 0:
            return full_in.at[rows_at(owner * rows_in + which * half_in + offset, size)]
        return full_out.at[rows_at(owner * rows_out + which * half_out + offset, size)]

    def own_piece(which, number):
        kind, offset, size = pieces[number]
        if kind == 0:
            return win_ref.at[rows_at(which * half_in + offset, size)]
        return wout_ref.at[rows_at(which * half_out + offset, size)]

    x_copies, y_copies, fx_copies, fy_copies = [], [], [], []
    for number in range(last):
        copy = remote(own_piece(mine, number), piece_of(m, mine, number), gather_send.at[1, number], gather_recv.at[1, number], x_peer)
        copy.start()
        x_copies.append(copy)
    whole_in = remote(win_ref, full_in.at[rows_at(m * rows_in, rows_in)], gather_send.at[0, 0], gather_recv.at[0, 0], core_peer)
    whole_out = remote(wout_ref, full_out.at[rows_at(m * rows_out, rows_out)], gather_send.at[0, 1], gather_recv.at[0, 1], core_peer)
    whole_in.start()
    whole_out.start()

    halo_size = sizes["halo"]
    halo_hit = lax.broadcasted_iota(jnp.int32, (count_nodes, 2 * halo_size), 0) == halo_ref[...].reshape(1, 2 * halo_size)
    item = lax.broadcasted_iota(jnp.int32, (2 * halo_size, 2 * padded), 0)
    place = item + jnp.where(item < halo_size, 0, padded - halo_size)
    spread = lax.broadcasted_iota(jnp.int32, (2 * halo_size, 2 * padded), 1) == place
    halo_hot = product(
        jnp.where(halo_hit, 1.0, 0.0).astype(bf16), jnp.where(spread, 1.0, 0.0).astype(bf16), (1, 0)
    ).astype(bf16)
    nodes = nodes_ref[...]
    nh, nl = split(nodes)
    nr = (nodes - nh.astype(f32) - nl.astype(f32)).astype(bf16)
    listed = product(halo_hot, nh, (0, 0)) + (product(halo_hot, nl, (0, 0)) + product(halo_hot, nr, (0, 0)))
    halo_send[0] = listed[:padded]
    halo_send[1] = listed[padded:]
    first_at, last_at = pl.ds(count_nodes, padded), pl.ds(count_nodes + padded, padded)
    to_next = remote(halo_send.at[0], table.at[first_at], halo_ssem.at[0], halo_rsem.at[0], next_peer)
    to_prev = remote(halo_send.at[1], table.at[last_at], halo_ssem.at[1], halo_rsem.at[1], prev_peer)
    to_next.start()
    to_prev.start()
    slots = count_nodes + 2 * padded
    table[0:count_nodes] = nodes
    table[slots : slots + count_nodes] = nodes

    senders = senders_ref[...].reshape(1, count_edges)
    senders = jnp.where(senders < count_nodes + halo_size, senders, senders + (padded - halo_size))
    receivers = receivers_ref[...].reshape(1, count_edges)
    targets = slots + jnp.minimum(receivers, count_nodes - 1)
    total_slots = slots + count_nodes
    index = lax.broadcasted_iota(jnp.int32, (total_slots, count_edges), 0)
    hot = jnp.where((index == senders) | (index == targets), 1.0, 0.0)
    hot_t = hot.astype(bf16)
    hot = jnp.transpose(hot).astype(bf16)
    keep = jnp.where((receivers < count_nodes) & (drop_ref[...].reshape(1, count_edges) == 1), f32(keep_scale), f32(0.0))
    keep = jnp.transpose(jnp.broadcast_to(keep, (128, count_edges)))[:, :1]

    for load in loads:
        load.wait()
    edges = split(edges_in[...])

    peer_x, peer_core, peer_far = 2 * far + c, 2 * x + (1 - c), 2 * far + (1 - c)

    def forward_x(number):
        x_copies[number].wait_recv()
        block = piece_of(peer_x, mine, number)
        copy = remote(block, block, gather_send.at[3, number], gather_recv.at[3, number], core_peer)
        if helped:
            along = remote(block, block, gather_send.at[2, number], gather_recv.at[2, number], y_peer)
            along.start()
            y_copies.append(along)
        copy.start()
        fx_copies.append(copy)

    def forward_y(number):
        if helped:
            y_copies[number].wait_recv()
            block = piece_of(peer_x, other, number)
            copy = remote(block, block, gather_send.at[4, number], gather_recv.at[4, number], core_peer)
            copy.start()
            fy_copies.append(copy)

    ahead = 2
    for number in range(count_in + ahead):
        if number < last:
            forward_x(number)
        if number >= ahead:
            forward_y(number - ahead)
    whole_in.wait_recv()
    to_next.wait_recv()
    to_prev.wait_recv()
    for number in range(count_in):
        fx_copies[number].wait_recv()
        if helped:
            fy_copies[number].wait_recv()

    w_a = split(full_in[0:depth])
    w_b = split(full_in[depth : 2 * depth])
    w_c = split(full_in[2 * depth : 3 * depth])
    table_pair = split(table[...])
    ends = jnp.concatenate(
        [
            product3(pick(table_pair, slice(0, slots)), w_b, (1, 0)),
            product3(pick(table_pair, slice(slots, total_slots)), w_c, (1, 0)),
        ],
        axis=0,
    )
    hidden_in = product3(edges, w_a, (1, 0)) + product2(hot, split(ends), (1, 0))
    gate = jax.nn.sigmoid(hidden_in)
    hidden = split(hidden_in * gate)
    slope = gate + hidden_in * gate * (1.0 - gate)

    for number in range(count_in, last):
        if number >= count_in + ahead:
            forward_x(number)
        forward_y(number)
    whole_out.wait_recv()
    for number in range(count_in, last):
        fx_copies[number].wait_recv()
        if helped:
            fy_copies[number].wait_recv()
    w_o = split(full_out[...])
    message = product3(hidden, w_o, (1, 0))
    centre = jnp.mean(message, axis=1, keepdims=True)
    variance = jnp.mean(message * message, axis=1, keepdims=True) - centre * centre
    scale = lax.rsqrt(variance + norm_epsilon)
    normed = (message - centre) * scale
    weighted = keep * cot[...]
    grad_message = split(
        scale
        * (
            weighted
            - jnp.mean(weighted, axis=1, keepdims=True)
            - normed * jnp.mean(weighted * normed, axis=1, keepdims=True)
        )
    )
    gout[...] = product3(hidden, grad_message, (0, 0))

    blocks, at, start = [], 0, 0
    for share in sizes["sum_out"]:
        size = rows_out * share // sum(sizes["sum_out"])
        blocks.append((1, start, pl.ds(at, size)))
        start, at = start + size, at + size
    first_in, start = len(blocks), 0
    for share in sizes["sum_in"]:
        size = rows_in * share // sum(sizes["sum_in"])
        blocks.append((0, start, pl.ds(at, size)))
        start, at = start + size, at + size

    def grad_rows(owner, number):
        kind, start, span = blocks[number]
        if kind == 1:
            return gout.at[rows_at(owner * rows_out + start, span.size)]
        return gin.at[rows_at(owner * rows_in + start, span.size)]

    core_copies, x_grad_copies = {}, {}

    def swap_cores(numbers):
        for side, owner in ((0, peer_far), (1, peer_core)):
            for number in numbers:
                copy = remote(
                    grad_rows(owner, number), from_core.at[side, blocks[number][2]],
                    core_ssem.at[side, number], core_rsem.at[side, number], core_peer,
                )
                copy.start()
                core_copies[side, number] = copy

    def swap_x(numbers):
        for number in numbers:
            core_copies[0, number].wait_recv()
            x_send[blocks[number][2]] = grad_rows(peer_x, number)[...] + from_core[0, blocks[number][2]]
            copy = remote(x_send.at[blocks[number][2]], from_x.at[blocks[number][2]], x_ssem.at[number], x_rsem.at[number], x_peer)
            copy.start()
            x_grad_copies[number] = copy

    early, late = range(first_in), range(first_in, len(blocks))
    swap_cores(early)
    grad_hidden = split(product3(grad_message, w_o, (1, 1)) * slope)
    swap_x(early)
    sums = product2(hot_t, grad_hidden, (1, 0))
    slot = lax.broadcasted_iota(jnp.int32, sums.shape, 0)
    gin[depth : 2 * depth] = product3(table_pair, split(jnp.where(slot < slots, sums, 0.0)), (0, 0))
    gin[2 * depth : 3 * depth] = product3(table_pair, split(jnp.where(slot < slots, 0.0, sums)), (0, 0))
    gin[0:depth] = product3(edges, grad_hidden, (0, 0))
    swap_cores(late)

    sums = split(sums)
    grad_table = product3(pick(sums, slice(0, slots)), w_b, (1, 1))
    back_send[0] = grad_table[count_nodes : count_nodes + padded]
    back_send[1] = grad_table[count_nodes + padded : slots]
    back_prev = remote(back_send.at[0], back_recv.at[pl.ds(0, padded)], halo_ssem.at[2], halo_rsem.at[2], prev_peer)
    back_next = remote(back_send.at[1], back_recv.at[pl.ds(padded, padded)], halo_ssem.at[3], halo_rsem.at[3], next_peer)
    back_prev.start()
    back_next.start()
    swap_x(late)
    own[...] = grad_table[:count_nodes] + product3(pick(sums, slice(slots, total_slots)), w_c, (1, 1))
    grad_edges[...] = cot[...] + product3(grad_hidden, w_a, (1, 1))
    edges_out = pltpu.make_async_copy(grad_edges, gedges_ref, local_sem.at[4])
    edges_out.start()

    def inward(number, to_mid):
        landing = (from_inner, inner_rsem) if to_mid else (from_outer, outer_rsem)
        return remote(acc.at[blocks[number][2]], landing[0].at[blocks[number][2]], inward_ssem.at[number], landing[1].at[number], inner_peer)

    def outward(number):
        return remote(total.at[blocks[number][2]], from_inner.at[blocks[number][2]], outward_ssem.at[number], inner_rsem.at[number], outer_peer)

    def collect(number):
        core_copies[1, number].wait_recv()
        x_grad_copies[number].wait_recv()
        acc[blocks[number][2]] = grad_rows(m, number)[...] + from_core[1, blocks[number][2]] + from_x[blocks[number][2]]

        @pl.when(has_outer)
        def _():
            inward(number, False).wait_recv()
            acc[blocks[number][2]] = acc[blocks[number][2]] + from_outer[blocks[number][2]]

        @pl.when(is_mid)
        def _():
            inward(number, True).start()

        @pl.when(jnp.logical_not(is_mid))
        def _():
            inward(number, False).start()

    factor = f32(sizes["factor"])

    def finish(number, sends):
        kind, start, span = blocks[number]
        inward(number, True).wait_recv()

        @pl.when(is_mid)
        def _():
            total[blocks[number][2]] = acc[blocks[number][2]] + from_inner[blocks[number][2]]

        @pl.when(jnp.logical_not(is_mid))
        def _():
            total[blocks[number][2]] = from_inner[blocks[number][2]]

        if sends:
            outward(number).start()
        result = gwout_ref if kind == 1 else gwin_ref
        result[pl.ds(start, span.size)] = total[blocks[number][2]] * factor

    lag = 2
    for number in range(len(blocks) + lag):
        if number < len(blocks):
            collect(number)
        if number == 4:
            back_prev.wait_recv()
            back_next.wait_recv()
            gnodes_ref[...] = own[...] + product2(halo_hot, split(back_recv[...]), (1, 0))
        if number >= lag:

            @pl.when(has_outer)
            def _():
                finish(number - lag, True)

    @pl.when(jnp.logical_not(has_outer))
    def _():
        for number in range(len(blocks)):
            finish(number, False)

    edges_out.wait()
    for copy in [whole_in, whole_out, to_next, to_prev, back_prev, back_next] + x_copies + y_copies + fx_copies + fy_copies:
        copy.wait_send()
    for number in range(len(blocks)):
        core_copies[0, number].wait_send()
        core_copies[1, number].wait_send()
        x_grad_copies[number].wait_send()
        inward(number, True).wait_send()

    @pl.when(has_outer)
    def _():
        for number in range(len(blocks)):
            outward(number).wait_send()


def body(mesh_shape, nodes, edges, senders, receivers, halo_rows, drop_mask, w_in, w_out, cotangent):
    count_nodes, depth = nodes.shape
    count_edges = edges.shape[0]
    halo_size = halo_rows.shape[0] // 2
    padded = -(-halo_size // 16) * 16
    doms = mesh_shape["dom"]
    sizes = {
        "groups": mesh_shape["groups"],
        "dom": doms,
        "gather_in": (3, 3, 3, 2, 1),
        "gather_out": (1, 1),
        "sum_out": (1, 1, 2, 4),
        "sum_in": (8, 8, 8, 8, 4, 4, 2, 2, 2, 1, 1),
        "halo": halo_size,
        "factor": 1.0 / math.sqrt(count_edges * doms * mesh_shape["mp"]),
    }
    vmem = pl.BlockSpec(memory_space=pltpu.VMEM)
    pieces = len(sizes["gather_in"]) + len(sizes["gather_out"])
    count = len(sizes["sum_in"]) + len(sizes["sum_out"])
    piece = (w_in.shape[0] + w_out.shape[0], depth)
    hbm = pl.BlockSpec(memory_space=pl.ANY)
    dma = pltpu.SemaphoreType.DMA
    return pl.pallas_call(
        functools.partial(kernel, sizes),
        out_shape=(
            jax.ShapeDtypeStruct(nodes.shape, f32),
            jax.ShapeDtypeStruct(edges.shape, f32),
            jax.ShapeDtypeStruct(w_in.shape, f32),
            jax.ShapeDtypeStruct(w_out.shape, f32),
        ),
        in_specs=[vmem, hbm, vmem, vmem, vmem, vmem, hbm, hbm, hbm],
        out_specs=(vmem, hbm, vmem, vmem),
        scratch_shapes=[
            pltpu.VMEM((2 * count_nodes + 2 * padded, depth), f32),
            pltpu.VMEM((3 * depth, depth), f32),
            pltpu.VMEM((depth, depth), f32),
            pltpu.VMEM((2, padded, depth), f32),
            pltpu.VMEM((2, padded, depth), f32),
            pltpu.VMEM((2 * padded, depth), f32),
            pltpu.VMEM((3 * depth, depth), f32),
            pltpu.VMEM((depth, depth), f32),
            pltpu.VMEM((2,) + piece, f32),
            pltpu.VMEM(piece, f32),
            pltpu.VMEM(piece, f32),
            pltpu.VMEM(piece, f32),
            pltpu.VMEM(piece, f32),
            pltpu.VMEM(piece, f32),
            pltpu.VMEM(piece, f32),
            dma((5, pieces)),
            dma((5, pieces)),
            dma((4,)),
            dma((4,)),
            dma((2, count)),
            dma((2, count)),
            dma((count,)),
            dma((count,)),
            dma((count,)),
            dma((count,)),
            dma((count,)),
            dma((count,)),
            pltpu.VMEM(edges.shape, f32),
            pltpu.VMEM(edges.shape, f32),
            pltpu.VMEM(edges.shape, f32),
            pltpu.VMEM(nodes.shape, f32),
            dma((5,)),
        ],
        compiler_params=pltpu.CompilerParams(
            collective_id=0, has_side_effects=True, vmem_limit_bytes=56 * 1024 * 1024
        ),
    )(
        nodes, edges, senders, receivers, halo_rows, drop_mask, w_in, w_out, cotangent
    )


def solution(mesh):
    return jax.shard_map(
        functools.partial(body, dict(mesh.shape)),
        mesh=mesh,
        in_specs=(
            P(("groups", "dom", "mp"), None),
            P(("groups", "dom", "mp"), None),
            P(("dom", "mp")),
            P(("dom", "mp")),
            P(("dom", "mp")),
            P(("dom", "mp")),
            P("mp", None),
            P("mp", None),
            P(("groups", "dom", "mp"), None),
        ),
        out_specs=(
            P(("groups", "dom", "mp"), None),
            P(("groups", "dom", "mp"), None),
            P(("groups", "mp"), None),
            P(("groups", "mp"), None),
        ),
        check_vma=False,
    )
```

```python
import functools
import math

import jax
import jax.numpy as jnp
from jax import lax
from jax.experimental import pallas as pl
from jax.experimental.pallas import tpu as pltpu
from jax.sharding import PartitionSpec as P

norm_epsilon = 1e-05
keep_scale = 1.0 / 0.9
MESH = pl.DeviceIdType.MESH
f32, bf16 = jnp.float32, jnp.bfloat16


def split(value):
    high = value.astype(bf16)
    return high, (value - high.astype(f32)).astype(bf16)


def product(left, right, contract):
    return lax.dot_general(left, right, ((contract[:1], contract[1:]), ((), ())), preferred_element_type=f32)


def product3(left, right, contract):
    (lh, ll), (rh, rl) = left, right
    return product(lh, rh, contract) + (product(lh, rl, contract) + product(ll, rh, contract))


def product2(exact, right, contract):
    rh, rl = right
    return product(exact, rh, contract) + product(exact, rl, contract)


def pick(pair, rows):
    return pair[0][rows], pair[1][rows]


def kernel(
    sizes,
    nodes_ref, edges_ref, senders_ref, receivers_ref, halo_ref, drop_ref, win_ref, wout_ref, cot_ref,
    gnodes_ref, gedges_ref, gwin_ref, gwout_ref,
    table, full_in, full_out, halo_send, back_send, back_recv, gin, gout,
    from_core, x_send, from_x, acc, from_outer, from_inner, total,
    gather_send, gather_recv, halo_ssem, halo_rsem, core_ssem, core_rsem, x_ssem, x_rsem,
    outer_rsem, inner_rsem, inward_ssem, outward_ssem,
    edges_in, cot, grad_edges, own, local_sem,
):
    groups, doms = sizes["groups"], sizes["dom"]
    count_parts = doms * 4
    g, d, m = lax.axis_index("groups"), lax.axis_index("dom"), lax.axis_index("mp")
    x, c = m // 2, m % 2
    far = 1 - x
    part = d * 4 + m
    after, before = (part + 1) % count_parts, (part + count_parts - 1) % count_parts
    core_peer = (g, d, 2 * x + (1 - c))
    x_peer = (g, d, 2 * far + c)
    y_peer = (1 - g, d, m)
    next_peer = (g, after // 4, after % 4)
    prev_peer = (g, before // 4, before % 4)
    left_half = d < doms // 2
    inner = jnp.where(left_half, d + 1, d - 1)
    outer = jnp.where(left_half, d - 1, d + 1)
    has_outer = (d > 0) & (d < doms - 1)
    is_mid = (d == doms // 2 - 1) | (d == doms // 2)
    inner_peer, outer_peer = (g, inner, m), (g, outer, m)
    helped = groups == 2

    loads = [
        pltpu.make_async_copy(edges_ref, edges_in, local_sem.at[0]),
        pltpu.make_async_copy(cot_ref, cot, local_sem.at[1]),
        pltpu.make_async_copy(win_ref, full_in.at[pl.ds(pl.multiple_of(m * win_ref.shape[0], 8), win_ref.shape[0])], local_sem.at[2]),
        pltpu.make_async_copy(wout_ref, full_out.at[pl.ds(pl.multiple_of(m * wout_ref.shape[0], 8), wout_ref.shape[0])], local_sem.at[3]),
    ]
    barrier = pltpu.get_barrier_semaphore()
    partners = [core_peer, x_peer, next_peer, prev_peer, inner_peer] + ([y_peer] if helped else [])
    for peer in partners:
        pl.semaphore_signal(barrier, inc=1, device_id=peer, device_id_type=MESH)

    @pl.when(has_outer)
    def _():
        pl.semaphore_signal(barrier, inc=1, device_id=outer_peer, device_id_type=MESH)
        pl.semaphore_wait(barrier, len(partners) + 1)

    @pl.when(jnp.logical_not(has_outer))
    def _():
        pl.semaphore_wait(barrier, len(partners))

    for load in loads:
        load.start()

    def remote(src, dst, send, recv, peer):
        return pltpu.make_async_remote_copy(
            src_ref=src, dst_ref=dst, send_sem=send, recv_sem=recv, device_id=peer, device_id_type=MESH
        )

    rows_in, rows_out = win_ref.shape[0], wout_ref.shape[0]
    depth = full_out.shape[0]
    count_nodes, count_edges = nodes_ref.shape[0], edges_ref.shape[0]
    padded = halo_send.shape[1]
    parts = 2 if helped else 1
    mine, other = (g, 1 - g) if helped else (0, 0)
    half_in, half_out = rows_in // parts, rows_out // parts
    pieces, start = [], 0
    for share in sizes["gather_in"]:
        pieces.append((0, start, half_in * share // sum(sizes["gather_in"])))
        start += pieces[-1][2]
    count_in, start = len(pieces), 0
    for share in sizes["gather_out"]:
        pieces.append((1, start, half_out * share // sum(sizes["gather_out"])))
        start += pieces[-1][2]
    last = len(pieces)

    def rows_at(start, size):
        return pl.ds(pl.multiple_of(start, 8), size)

    def piece_of(owner, which, number):
        kind, offset, size = pieces[number]
        if kind == 0:
            return full_in.at[rows_at(owner * rows_in + which * half_in + offset, size)]
        return full_out.at[rows_at(owner * rows_out + which * half_out + offset, size)]

    def own_piece(which, number):
        kind, offset, size = pieces[number]
        if kind == 0:
            return win_ref.at[rows_at(which * half_in + offset, size)]
        return wout_ref.at[rows_at(which * half_out + offset, size)]

    x_copies, y_copies, fx_copies, fy_copies = [], [], [], []
    for number in range(last):
        copy = remote(own_piece(mine, number), piece_of(m, mine, number), gather_send.at[1, number], gather_recv.at[1, number], x_peer)
        copy.start()
        x_copies.append(copy)
    whole_in = remote(win_ref, full_in.at[rows_at(m * rows_in, rows_in)], gather_send.at[0, 0], gather_recv.at[0, 0], core_peer)
    whole_out = remote(wout_ref, full_out.at[rows_at(m * rows_out, rows_out)], gather_send.at[0, 1], gather_recv.at[0, 1], core_peer)
    whole_in.start()
    whole_out.start()

    halo_size = sizes["halo"]
    halo_hit = lax.broadcasted_iota(jnp.int32, (count_nodes, 2 * halo_size), 0) == halo_ref[...].reshape(1, 2 * halo_size)
    item = lax.broadcasted_iota(jnp.int32, (2 * halo_size, 2 * padded), 0)
    place = item + jnp.where(item < halo_size, 0, padded - halo_size)
    spread = lax.broadcasted_iota(jnp.int32, (2 * halo_size, 2 * padded), 1) == place
    halo_hot = product(
        jnp.where(halo_hit, 1.0, 0.0).astype(bf16), jnp.where(spread, 1.0, 0.0).astype(bf16), (1, 0)
    ).astype(bf16)
    nodes = nodes_ref[...]
    nh, nl = split(nodes)
    nr = (nodes - nh.astype(f32) - nl.astype(f32)).astype(bf16)
    listed = product(halo_hot, nh, (0, 0)) + (product(halo_hot, nl, (0, 0)) + product(halo_hot, nr, (0, 0)))
    halo_send[0] = listed[:padded]
    halo_send[1] = listed[padded:]
    first_at, last_at = pl.ds(count_nodes, padded), pl.ds(count_nodes + padded, padded)
    to_next = remote(halo_send.at[0], table.at[first_at], halo_ssem.at[0], halo_rsem.at[0], next_peer)
    to_prev = remote(halo_send.at[1], table.at[last_at], halo_ssem.at[1], halo_rsem.at[1], prev_peer)
    to_next.start()
    to_prev.start()
    slots = count_nodes + 2 * padded
    table[0:count_nodes] = nodes
    table[slots : slots + count_nodes] = nodes

    senders = senders_ref[...].reshape(1, count_edges)
    senders = jnp.where(senders < count_nodes + halo_size, senders, senders + (padded - halo_size))
    receivers = receivers_ref[...].reshape(1, count_edges)
    targets = slots + jnp.minimum(receivers, count_nodes - 1)
    total_slots = slots + count_nodes
    index = lax.broadcasted_iota(jnp.int32, (total_slots, count_edges), 0)
    hot = jnp.where((index == senders) | (index == targets), 1.0, 0.0)
    hot_t = hot.astype(bf16)
    hot = jnp.transpose(hot).astype(bf16)
    keep = jnp.where((receivers < count_nodes) & (drop_ref[...].reshape(1, count_edges) == 1), f32(keep_scale), f32(0.0))
    keep = jnp.transpose(jnp.broadcast_to(keep, (128, count_edges)))[:, :1]

    for load in loads:
        load.wait()
    edges = split(edges_in[...])

    peer_x, peer_core, peer_far = 2 * far + c, 2 * x + (1 - c), 2 * far + (1 - c)

    def forward_x(number):
        x_copies[number].wait_recv()
        block = piece_of(peer_x, mine, number)
        copy = remote(block, block, gather_send.at[3, number], gather_recv.at[3, number], core_peer)
        if helped:
            along = remote(block, block, gather_send.at[2, number], gather_recv.at[2, number], y_peer)
            along.start()
            y_copies.append(along)
        copy.start()
        fx_copies.append(copy)

    def forward_y(number):
        if helped:
            y_copies[number].wait_recv()
            block = piece_of(peer_x, other, number)
            copy = remote(block, block, gather_send.at[4, number], gather_recv.at[4, number], core_peer)
            copy.start()
            fy_copies.append(copy)

    ahead = 2
    for number in range(count_in + ahead):
        if number < last:
            forward_x(number)
        if number >= ahead:
            forward_y(number - ahead)
    whole_in.wait_recv()
    to_next.wait_recv()
    to_prev.wait_recv()
    for number in range(count_in):
        fx_copies[number].wait_recv()
        if helped:
            fy_copies[number].wait_recv()

    w_a = split(full_in[0:depth])
    w_b = split(full_in[depth : 2 * depth])
    w_c = split(full_in[2 * depth : 3 * depth])
    table_pair = split(table[...])
    ends = jnp.concatenate(
        [
            product3(pick(table_pair, slice(0, slots)), w_b, (1, 0)),
            product3(pick(table_pair, slice(slots, total_slots)), w_c, (1, 0)),
        ],
        axis=0,
    )
    hidden_in = product3(edges, w_a, (1, 0)) + product2(hot, split(ends), (1, 0))
    gate = jax.nn.sigmoid(hidden_in)
    hidden = split(hidden_in * gate)
    slope = gate + hidden_in * gate * (1.0 - gate)

    for number in range(count_in, last):
        if number >= count_in + ahead:
            forward_x(number)
        forward_y(number)
    whole_out.wait_recv()
    for number in range(count_in, last):
        fx_copies[number].wait_recv()
        if helped:
            fy_copies[number].wait_recv()
    w_o = split(full_out[...])
    message = product3(hidden, w_o, (1, 0))
    centre = jnp.mean(message, axis=1, keepdims=True)
    variance = jnp.mean(message * message, axis=1, keepdims=True) - centre * centre
    scale = lax.rsqrt(variance + norm_epsilon)
    normed = (message - centre) * scale
    weighted = keep * cot[...]
    grad_message = split(
        scale
        * (
            weighted
            - jnp.mean(weighted, axis=1, keepdims=True)
            - normed * jnp.mean(weighted * normed, axis=1, keepdims=True)
        )
    )
    gout[...] = product3(hidden, grad_message, (0, 0))

    blocks, at, start = [], 0, 0
    for share in sizes["sum_out"]:
        size = rows_out * share // sum(sizes["sum_out"])
        blocks.append((1, start, pl.ds(at, size)))
        start, at = start + size, at + size
    first_in, start = len(blocks), 0
    for share in sizes["sum_in"]:
        size = rows_in * share // sum(sizes["sum_in"])
        blocks.append((0, start, pl.ds(at, size)))
        start, at = start + size, at + size

    def grad_rows(owner, number):
        kind, start, span = blocks[number]
        if kind == 1:
            return gout.at[rows_at(owner * rows_out + start, span.size)]
        return gin.at[rows_at(owner * rows_in + start, span.size)]

    core_copies, x_grad_copies = {}, {}

    def swap_cores(numbers):
        for side, owner in ((0, peer_far), (1, peer_core)):
            for number in numbers:
                copy = remote(
                    grad_rows(owner, number), from_core.at[side, blocks[number][2]],
                    core_ssem.at[side, number], core_rsem.at[side, number], core_peer,
                )
                copy.start()
                core_copies[side, number] = copy

    def swap_x(numbers):
        for number in numbers:
            core_copies[0, number].wait_recv()
            x_send[blocks[number][2]] = grad_rows(peer_x, number)[...] + from_core[0, blocks[number][2]]
            copy = remote(x_send.at[blocks[number][2]], from_x.at[blocks[number][2]], x_ssem.at[number], x_rsem.at[number], x_peer)
            copy.start()
            x_grad_copies[number] = copy

    early, late = range(first_in), range(first_in, len(blocks))
    swap_cores(early)
    grad_hidden = split(product3(grad_message, w_o, (1, 1)) * slope)
    swap_x(early)
    sums = product2(hot_t, grad_hidden, (1, 0))
    slot = lax.broadcasted_iota(jnp.int32, sums.shape, 0)
    gin[depth : 2 * depth] = product3(table_pair, split(jnp.where(slot < slots, sums, 0.0)), (0, 0))
    gin[2 * depth : 3 * depth] = product3(table_pair, split(jnp.where(slot < slots, 0.0, sums)), (0, 0))
    gin[0:depth] = product3(edges, grad_hidden, (0, 0))
    swap_cores(late)

    sums = split(sums)
    grad_table = product3(pick(sums, slice(0, slots)), w_b, (1, 1))
    back_send[0] = grad_table[count_nodes : count_nodes + padded]
    back_send[1] = grad_table[count_nodes + padded : slots]
    back_prev = remote(back_send.at[0], back_recv.at[pl.ds(0, padded)], halo_ssem.at[2], halo_rsem.at[2], prev_peer)
    back_next = remote(back_send.at[1], back_recv.at[pl.ds(padded, padded)], halo_ssem.at[3], halo_rsem.at[3], next_peer)
    back_prev.start()
    back_next.start()
    swap_x(late)
    own[...] = grad_table[:count_nodes] + product3(pick(sums, slice(slots, total_slots)), w_c, (1, 1))
    grad_edges[...] = cot[...] + product3(grad_hidden, w_a, (1, 1))
    edges_out = pltpu.make_async_copy(grad_edges, gedges_ref, local_sem.at[4])
    edges_out.start()

    def inward(number, to_mid):
        landing = (from_inner, inner_rsem) if to_mid else (from_outer, outer_rsem)
        return remote(acc.at[blocks[number][2]], landing[0].at[blocks[number][2]], inward_ssem.at[number], landing[1].at[number], inner_peer)

    def outward(number):
        return remote(total.at[blocks[number][2]], from_inner.at[blocks[number][2]], outward_ssem.at[number], inner_rsem.at[number], outer_peer)

    def collect(number):
        core_copies[1, number].wait_recv()
        x_grad_copies[number].wait_recv()
        acc[blocks[number][2]] = grad_rows(m, number)[...] + from_core[1, blocks[number][2]] + from_x[blocks[number][2]]

        @pl.when(has_outer)
        def _():
            inward(number, False).wait_recv()
            acc[blocks[number][2]] = acc[blocks[number][2]] + from_outer[blocks[number][2]]

        @pl.when(is_mid)
        def _():
            inward(number, True).start()

        @pl.when(jnp.logical_not(is_mid))
        def _():
            inward(number, False).start()

    factor = f32(sizes["factor"])

    def finish(number, sends):
        kind, start, span = blocks[number]
        inward(number, True).wait_recv()

        @pl.when(is_mid)
        def _():
            total[blocks[number][2]] = acc[blocks[number][2]] + from_inner[blocks[number][2]]

        @pl.when(jnp.logical_not(is_mid))
        def _():
            total[blocks[number][2]] = from_inner[blocks[number][2]]

        if sends:
            outward(number).start()
        result = gwout_ref if kind == 1 else gwin_ref
        result[pl.ds(start, span.size)] = total[blocks[number][2]] * factor

    ends_at = [span.start + span.size for _, _, span in blocks]
    done = 0
    for number in range(len(blocks)):
        collect(number)
        if number == first_in:
            back_prev.wait_recv()
            back_next.wait_recv()
            gnodes_ref[...] = own[...] + product2(halo_hot, split(back_recv[...]), (1, 0))
        ready = done
        while ready < len(blocks) and ends_at[number] - ends_at[ready] >= sizes["lag"]:
            ready += 1
        if number == len(blocks) - 1:
            ready = len(blocks)

        @pl.when(has_outer)
        def _():
            for earlier in range(done, ready):
                finish(earlier, True)

        done = ready

    @pl.when(jnp.logical_not(has_outer))
    def _():
        for number in range(len(blocks)):
            finish(number, False)

    edges_out.wait()
    for copy in [whole_in, whole_out, to_next, to_prev, back_prev, back_next] + x_copies + y_copies + fx_copies + fy_copies:
        copy.wait_send()
    for number in range(len(blocks)):
        core_copies[0, number].wait_send()
        core_copies[1, number].wait_send()
        x_grad_copies[number].wait_send()
        inward(number, True).wait_send()

    @pl.when(has_outer)
    def _():
        for number in range(len(blocks)):
            outward(number).wait_send()


emit_pieces = 4


def emit(*refs):
    copies = []
    for number in range(4):
        source, target = refs[number], refs[4 + number]
        size = source.shape[0] // emit_pieces
        if size % 8:
            spans = [pl.ds(0, source.shape[0])]
        else:
            spans = [pl.ds(start, size) for start in range(0, source.shape[0], size)]
        for place, span in enumerate(spans):
            copies.append(
                (
                    pltpu.make_async_copy(source.at[span], refs[8 + number].at[span], refs[12].at[number, place]),
                    pltpu.make_async_copy(refs[8 + number].at[span], target.at[span], refs[13].at[number, place]),
                )
            )
    for load, _ in copies:
        load.start()
    for load, store in copies:
        load.wait()
        store.start()
    for _, store in copies:
        store.wait()


def body(mesh_shape, nodes, edges, senders, receivers, halo_rows, drop_mask, w_in, w_out, cotangent):
    count_nodes, depth = nodes.shape
    count_edges = edges.shape[0]
    halo_size = halo_rows.shape[0] // 2
    padded = -(-halo_size // 16) * 16
    doms = mesh_shape["dom"]
    sizes = {
        "groups": mesh_shape["groups"],
        "dom": doms,
        "gather_in": (3, 3, 3, 2, 1),
        "gather_out": (1, 1),
        "lag": 64,
        "sum_out": (1, 1, 1, 1),
        "sum_in": (4, 4, 4, 4, 4, 4, 4, 4, 4, 4, 2, 2, 2, 1, 1),
        "halo": halo_size,
        "factor": 1.0 / math.sqrt(count_edges * doms * mesh_shape["mp"]),
    }
    vmem = pl.BlockSpec(memory_space=pltpu.VMEM)
    pieces = len(sizes["gather_in"]) + len(sizes["gather_out"])
    count = len(sizes["sum_in"]) + len(sizes["sum_out"])
    piece = (w_in.shape[0] + w_out.shape[0], depth)
    hbm = pl.BlockSpec(memory_space=pl.ANY)
    dma = pltpu.SemaphoreType.DMA
    results = pl.pallas_call(
        functools.partial(kernel, sizes),
        out_shape=(
            jax.ShapeDtypeStruct(nodes.shape, f32),
            jax.ShapeDtypeStruct(edges.shape, f32),
            jax.ShapeDtypeStruct(w_in.shape, f32),
            jax.ShapeDtypeStruct(w_out.shape, f32),
        ),
        in_specs=[vmem, hbm, vmem, vmem, vmem, vmem, hbm, hbm, hbm],
        out_specs=(vmem, hbm, vmem, vmem),
        scratch_shapes=[
            pltpu.VMEM((2 * count_nodes + 2 * padded, depth), f32),
            pltpu.VMEM((3 * depth, depth), f32),
            pltpu.VMEM((depth, depth), f32),
            pltpu.VMEM((2, padded, depth), f32),
            pltpu.VMEM((2, padded, depth), f32),
            pltpu.VMEM((2 * padded, depth), f32),
            pltpu.VMEM((3 * depth, depth), f32),
            pltpu.VMEM((depth, depth), f32),
            pltpu.VMEM((2,) + piece, f32),
            pltpu.VMEM(piece, f32),
            pltpu.VMEM(piece, f32),
            pltpu.VMEM(piece, f32),
            pltpu.VMEM(piece, f32),
            pltpu.VMEM(piece, f32),
            pltpu.VMEM(piece, f32),
            dma((5, pieces)),
            dma((5, pieces)),
            dma((4,)),
            dma((4,)),
            dma((2, count)),
            dma((2, count)),
            dma((count,)),
            dma((count,)),
            dma((count,)),
            dma((count,)),
            dma((count,)),
            dma((count,)),
            pltpu.VMEM(edges.shape, f32),
            pltpu.VMEM(edges.shape, f32),
            pltpu.VMEM(edges.shape, f32),
            pltpu.VMEM(nodes.shape, f32),
            dma((5,)),
        ],
        compiler_params=pltpu.CompilerParams(
            collective_id=0, has_side_effects=True, vmem_limit_bytes=56 * 1024 * 1024
        ),
    )(
        nodes, edges, senders, receivers, halo_rows, drop_mask, w_in, w_out, cotangent
    )
    return pl.pallas_call(
        emit,
        out_shape=tuple(jax.ShapeDtypeStruct(result.shape, f32) for result in results),
        in_specs=[hbm] * 4,
        out_specs=(hbm,) * 4,
        scratch_shapes=[pltpu.VMEM(result.shape, f32) for result in results] + [dma((4, emit_pieces))] * 2,
    )(*results)


def solution(mesh):
    return jax.shard_map(
        functools.partial(body, dict(mesh.shape)),
        mesh=mesh,
        in_specs=(
            P(("groups", "dom", "mp"), None),
            P(("groups", "dom", "mp"), None),
            P(("dom", "mp")),
            P(("dom", "mp")),
            P(("dom", "mp")),
            P(("dom", "mp")),
            P("mp", None),
            P("mp", None),
            P(("groups", "dom", "mp"), None),
        ),
        out_specs=(
            P(("groups", "dom", "mp"), None),
            P(("groups", "dom", "mp"), None),
            P(("groups", "mp"), None),
            P(("groups", "mp"), None),
        ),
        check_vma=False,
    )
```

```python
import functools
import math

import jax
import jax.numpy as jnp
from jax import lax
from jax.experimental import pallas as pl
from jax.experimental.pallas import tpu as pltpu
from jax.sharding import PartitionSpec as P

norm_epsilon = 1e-05
keep_scale = 1.0 / 0.9
MESH = pl.DeviceIdType.MESH
f32, bf16 = jnp.float32, jnp.bfloat16


def split(value):
    high = value.astype(bf16)
    return high, (value - high.astype(f32)).astype(bf16)


def product(left, right, contract):
    return lax.dot_general(left, right, ((contract[:1], contract[1:]), ((), ())), preferred_element_type=f32)


def product3(left, right, contract):
    (lh, ll), (rh, rl) = left, right
    return product(lh, rh, contract) + (product(lh, rl, contract) + product(ll, rh, contract))


def product2(exact, right, contract):
    rh, rl = right
    return product(exact, rh, contract) + product(exact, rl, contract)


def pick(pair, rows):
    return pair[0][rows], pair[1][rows]


def kernel(
    sizes,
    nodes_ref, edges_ref, senders_ref, receivers_ref, halo_ref, drop_ref, win_ref, wout_ref, cot_ref,
    gnodes_ref, gedges_ref, gwin_ref, gwout_ref,
    table, full_in, full_out, halo_send, back_send, back_recv, gin, gout,
    from_core, x_send, from_x, acc, from_outer, from_inner, total,
    gather_send, gather_recv, halo_ssem, halo_rsem, core_ssem, core_rsem, x_ssem, x_rsem,
    outer_rsem, inner_rsem, inward_ssem, outward_ssem,
    edges_in, cot, grad_edges, own, local_sem,
):
    groups, doms = sizes["groups"], sizes["dom"]
    count_parts = doms * 4
    g, d, m = lax.axis_index("groups"), lax.axis_index("dom"), lax.axis_index("mp")
    x, c = m // 2, m % 2
    far = 1 - x
    part = d * 4 + m
    after, before = (part + 1) % count_parts, (part + count_parts - 1) % count_parts
    core_peer = (g, d, 2 * x + (1 - c))
    x_peer = (g, d, 2 * far + c)
    y_peer = (1 - g, d, m)
    next_peer = (g, after // 4, after % 4)
    prev_peer = (g, before // 4, before % 4)
    left_half = d < doms // 2
    inner = jnp.where(left_half, d + 1, d - 1)
    outer = jnp.where(left_half, d - 1, d + 1)
    has_outer = (d > 0) & (d < doms - 1)
    is_mid = (d == doms // 2 - 1) | (d == doms // 2)
    inner_peer, outer_peer = (g, inner, m), (g, outer, m)
    helped = groups == 2

    loads = [
        pltpu.make_async_copy(edges_ref, edges_in, local_sem.at[0]),
        pltpu.make_async_copy(cot_ref, cot, local_sem.at[1]),
        pltpu.make_async_copy(win_ref, full_in.at[pl.ds(pl.multiple_of(m * win_ref.shape[0], 8), win_ref.shape[0])], local_sem.at[2]),
        pltpu.make_async_copy(wout_ref, full_out.at[pl.ds(pl.multiple_of(m * wout_ref.shape[0], 8), wout_ref.shape[0])], local_sem.at[3]),
    ]
    barrier = pltpu.get_barrier_semaphore()
    partners = [core_peer, x_peer, next_peer, prev_peer, inner_peer] + ([y_peer] if helped else [])
    for peer in partners:
        pl.semaphore_signal(barrier, inc=1, device_id=peer, device_id_type=MESH)

    @pl.when(has_outer)
    def _():
        pl.semaphore_signal(barrier, inc=1, device_id=outer_peer, device_id_type=MESH)
        pl.semaphore_wait(barrier, len(partners) + 1)

    @pl.when(jnp.logical_not(has_outer))
    def _():
        pl.semaphore_wait(barrier, len(partners))

    for load in loads:
        load.start()

    def remote(src, dst, send, recv, peer):
        return pltpu.make_async_remote_copy(
            src_ref=src, dst_ref=dst, send_sem=send, recv_sem=recv, device_id=peer, device_id_type=MESH
        )

    rows_in, rows_out = win_ref.shape[0], wout_ref.shape[0]
    depth = full_out.shape[0]
    count_nodes, count_edges = nodes_ref.shape[0], edges_ref.shape[0]
    padded = halo_send.shape[1]
    parts = 2 if helped else 1
    mine, other = (g, 1 - g) if helped else (0, 0)
    half_in, half_out = rows_in // parts, rows_out // parts
    pieces, start = [], 0
    for share in sizes["gather_in"]:
        pieces.append((0, start, half_in * share // sum(sizes["gather_in"])))
        start += pieces[-1][2]
    count_in, start = len(pieces), 0
    for share in sizes["gather_out"]:
        pieces.append((1, start, half_out * share // sum(sizes["gather_out"])))
        start += pieces[-1][2]
    last = len(pieces)

    def rows_at(start, size):
        return pl.ds(pl.multiple_of(start, 8), size)

    def piece_of(owner, which, number):
        kind, offset, size = pieces[number]
        if kind == 0:
            return full_in.at[rows_at(owner * rows_in + which * half_in + offset, size)]
        return full_out.at[rows_at(owner * rows_out + which * half_out + offset, size)]

    def own_piece(which, number):
        kind, offset, size = pieces[number]
        if kind == 0:
            return win_ref.at[rows_at(which * half_in + offset, size)]
        return wout_ref.at[rows_at(which * half_out + offset, size)]

    x_copies, y_copies, fx_copies, fy_copies = [], [], [], []
    for number in range(last):
        copy = remote(own_piece(mine, number), piece_of(m, mine, number), gather_send.at[1, number], gather_recv.at[1, number], x_peer)
        copy.start()
        x_copies.append(copy)
    whole_in = remote(win_ref, full_in.at[rows_at(m * rows_in, rows_in)], gather_send.at[0, 0], gather_recv.at[0, 0], core_peer)
    whole_out = remote(wout_ref, full_out.at[rows_at(m * rows_out, rows_out)], gather_send.at[0, 1], gather_recv.at[0, 1], core_peer)
    whole_in.start()
    whole_out.start()

    halo_size = sizes["halo"]
    halo_hit = lax.broadcasted_iota(jnp.int32, (count_nodes, 2 * halo_size), 0) == halo_ref[...].reshape(1, 2 * halo_size)
    item = lax.broadcasted_iota(jnp.int32, (2 * halo_size, 2 * padded), 0)
    place = item + jnp.where(item < halo_size, 0, padded - halo_size)
    spread = lax.broadcasted_iota(jnp.int32, (2 * halo_size, 2 * padded), 1) == place
    halo_hot = product(
        jnp.where(halo_hit, 1.0, 0.0).astype(bf16), jnp.where(spread, 1.0, 0.0).astype(bf16), (1, 0)
    ).astype(bf16)
    nodes = nodes_ref[...]
    nh, nl = split(nodes)
    nr = (nodes - nh.astype(f32) - nl.astype(f32)).astype(bf16)
    listed = product(halo_hot, nh, (0, 0)) + (product(halo_hot, nl, (0, 0)) + product(halo_hot, nr, (0, 0)))
    halo_send[0] = listed[:padded]
    halo_send[1] = listed[padded:]
    first_at, last_at = pl.ds(count_nodes, padded), pl.ds(count_nodes + padded, padded)
    to_next = remote(halo_send.at[0], table.at[first_at], halo_ssem.at[0], halo_rsem.at[0], next_peer)
    to_prev = remote(halo_send.at[1], table.at[last_at], halo_ssem.at[1], halo_rsem.at[1], prev_peer)
    to_next.start()
    to_prev.start()
    slots = count_nodes + 2 * padded
    table[0:count_nodes] = nodes
    table[slots : slots + count_nodes] = nodes

    peer_x, peer_core, peer_far = 2 * far + c, 2 * x + (1 - c), 2 * far + (1 - c)

    def forward_x(number):
        x_copies[number].wait_recv()
        block = piece_of(peer_x, mine, number)
        copy = remote(block, block, gather_send.at[3, number], gather_recv.at[3, number], core_peer)
        if helped:
            along = remote(block, block, gather_send.at[2, number], gather_recv.at[2, number], y_peer)
            along.start()
            y_copies.append(along)
        copy.start()
        fx_copies.append(copy)

    def forward_y(number):
        if helped:
            y_copies[number].wait_recv()
            block = piece_of(peer_x, other, number)
            copy = remote(block, block, gather_send.at[4, number], gather_recv.at[4, number], core_peer)
            copy.start()
            fy_copies.append(copy)

    ahead = 2
    forward_x(0)
    senders = senders_ref[...].reshape(1, count_edges)
    senders = jnp.where(senders < count_nodes + halo_size, senders, senders + (padded - halo_size))
    receivers = receivers_ref[...].reshape(1, count_edges)
    targets = slots + jnp.minimum(receivers, count_nodes - 1)
    total_slots = slots + count_nodes
    index = lax.broadcasted_iota(jnp.int32, (total_slots, count_edges), 0)
    hot = jnp.where((index == senders) | (index == targets), 1.0, 0.0)
    hot_t = hot.astype(bf16)
    hot = jnp.transpose(hot).astype(bf16)
    forward_x(1)
    keep = jnp.where((receivers < count_nodes) & (drop_ref[...].reshape(1, count_edges) == 1), f32(keep_scale), f32(0.0))
    keep = jnp.transpose(jnp.broadcast_to(keep, (128, count_edges)))[:, :1]

    forward_x(2)
    forward_y(0)
    for load in loads:
        load.wait()
    edges = split(edges_in[...])

    for number in range(ahead + 1, count_in + ahead):
        if number < last:
            forward_x(number)
        forward_y(number - ahead)
    whole_in.wait_recv()
    to_next.wait_recv()
    to_prev.wait_recv()
    for number in range(count_in):
        fx_copies[number].wait_recv()
        if helped:
            fy_copies[number].wait_recv()

    w_a = split(full_in[0:depth])
    w_b = split(full_in[depth : 2 * depth])
    w_c = split(full_in[2 * depth : 3 * depth])
    table_pair = split(table[...])
    ends = jnp.concatenate(
        [
            product3(pick(table_pair, slice(0, slots)), w_b, (1, 0)),
            product3(pick(table_pair, slice(slots, total_slots)), w_c, (1, 0)),
        ],
        axis=0,
    )
    hidden_in = product3(edges, w_a, (1, 0)) + product2(hot, split(ends), (1, 0))
    gate = jax.nn.sigmoid(hidden_in)
    hidden = split(hidden_in * gate)
    slope = gate + hidden_in * gate * (1.0 - gate)

    for number in range(count_in, last):
        if number >= count_in + ahead:
            forward_x(number)
        forward_y(number)
    whole_out.wait_recv()
    for number in range(count_in, last):
        fx_copies[number].wait_recv()
        if helped:
            fy_copies[number].wait_recv()
    w_o = split(full_out[...])
    message = product3(hidden, w_o, (1, 0))
    centre = jnp.mean(message, axis=1, keepdims=True)
    variance = jnp.mean(message * message, axis=1, keepdims=True) - centre * centre
    scale = lax.rsqrt(variance + norm_epsilon)
    normed = (message - centre) * scale
    weighted = keep * cot[...]
    grad_message = split(
        scale
        * (
            weighted
            - jnp.mean(weighted, axis=1, keepdims=True)
            - normed * jnp.mean(weighted * normed, axis=1, keepdims=True)
        )
    )
    gout[...] = product3(hidden, grad_message, (0, 0))

    blocks, at, start = [], 0, 0
    for share in sizes["sum_out"]:
        size = rows_out * share // sum(sizes["sum_out"])
        blocks.append((1, start, pl.ds(at, size)))
        start, at = start + size, at + size
    first_in, start = len(blocks), 0
    for share in sizes["sum_in"]:
        size = rows_in * share // sum(sizes["sum_in"])
        blocks.append((0, start, pl.ds(at, size)))
        start, at = start + size, at + size

    def grad_rows(owner, number):
        kind, start, span = blocks[number]
        if kind == 1:
            return gout.at[rows_at(owner * rows_out + start, span.size)]
        return gin.at[rows_at(owner * rows_in + start, span.size)]

    core_copies, x_grad_copies = {}, {}

    def swap_cores(numbers):
        for side, owner in ((0, peer_far), (1, peer_core)):
            for number in numbers:
                copy = remote(
                    grad_rows(owner, number), from_core.at[side, blocks[number][2]],
                    core_ssem.at[side, number], core_rsem.at[side, number], core_peer,
                )
                copy.start()
                core_copies[side, number] = copy

    def swap_x(numbers):
        for number in numbers:
            core_copies[0, number].wait_recv()
            x_send[blocks[number][2]] = grad_rows(peer_x, number)[...] + from_core[0, blocks[number][2]]
            copy = remote(x_send.at[blocks[number][2]], from_x.at[blocks[number][2]], x_ssem.at[number], x_rsem.at[number], x_peer)
            copy.start()
            x_grad_copies[number] = copy

    def inward(number, to_mid):
        landing = (from_inner, inner_rsem) if to_mid else (from_outer, outer_rsem)
        return remote(acc.at[blocks[number][2]], landing[0].at[blocks[number][2]], inward_ssem.at[number], landing[1].at[number], inner_peer)

    def outward(number):
        return remote(total.at[blocks[number][2]], from_inner.at[blocks[number][2]], outward_ssem.at[number], inner_rsem.at[number], outer_peer)

    def gather(number):
        core_copies[1, number].wait_recv()
        x_grad_copies[number].wait_recv()
        acc[blocks[number][2]] = grad_rows(m, number)[...] + from_core[1, blocks[number][2]] + from_x[blocks[number][2]]

        @pl.when(jnp.logical_not(has_outer))
        def _():
            pass_inward(number)

    def pass_inward(number):
        @pl.when(is_mid)
        def _():
            inward(number, True).start()

        @pl.when(jnp.logical_not(is_mid))
        def _():
            inward(number, False).start()

    def collect(number):
        @pl.when(has_outer)
        def _():
            inward(number, False).wait_recv()
            acc[blocks[number][2]] = acc[blocks[number][2]] + from_outer[blocks[number][2]]
            pass_inward(number)

    factor = f32(sizes["factor"])

    def finish(number, sends):
        kind, start, span = blocks[number]
        inward(number, True).wait_recv()

        @pl.when(is_mid)
        def _():
            total[blocks[number][2]] = acc[blocks[number][2]] + from_inner[blocks[number][2]]

        @pl.when(jnp.logical_not(is_mid))
        def _():
            total[blocks[number][2]] = from_inner[blocks[number][2]]

        if sends:
            outward(number).start()
        result = gwout_ref if kind == 1 else gwin_ref
        result[pl.ds(start, span.size)] = total[blocks[number][2]] * factor

    early, late = range(first_in), range(first_in, len(blocks))
    swap_cores(early)
    grad_hidden = split(product3(grad_message, w_o, (1, 1)) * slope)
    swap_x(early)
    sums = product2(hot_t, grad_hidden, (1, 0))
    slot = lax.broadcasted_iota(jnp.int32, sums.shape, 0)
    gin[depth : 2 * depth] = product3(table_pair, split(jnp.where(slot < slots, sums, 0.0)), (0, 0))
    gin[2 * depth : 3 * depth] = product3(table_pair, split(jnp.where(slot < slots, 0.0, sums)), (0, 0))
    gin[0:depth] = product3(edges, grad_hidden, (0, 0))
    swap_cores(late)
    begun = 2
    for number in range(begun):
        gather(number)

    sums = split(sums)
    grad_table = product3(pick(sums, slice(0, slots)), w_b, (1, 1))
    back_send[0] = grad_table[count_nodes : count_nodes + padded]
    back_send[1] = grad_table[count_nodes + padded : slots]
    back_prev = remote(back_send.at[0], back_recv.at[pl.ds(0, padded)], halo_ssem.at[2], halo_rsem.at[2], prev_peer)
    back_next = remote(back_send.at[1], back_recv.at[pl.ds(padded, padded)], halo_ssem.at[3], halo_rsem.at[3], next_peer)
    back_prev.start()
    back_next.start()
    swap_x(late)
    own[...] = grad_table[:count_nodes] + product3(pick(sums, slice(slots, total_slots)), w_c, (1, 1))
    grad_edges[...] = cot[...] + product3(grad_hidden, w_a, (1, 1))
    edges_out = pltpu.make_async_copy(grad_edges, gedges_ref, local_sem.at[4])
    edges_out.start()

    ends_at = [span.start + span.size for _, _, span in blocks]
    done = 0
    for number in range(len(blocks)):
        if number >= begun:
            gather(number)
        collect(number)
        if number == first_in:
            back_prev.wait_recv()
            back_next.wait_recv()
            gnodes_ref[...] = own[...] + product2(halo_hot, split(back_recv[...]), (1, 0))
        ready = done
        while ready < len(blocks) and ends_at[number] - ends_at[ready] >= sizes["lag"]:
            ready += 1
        if number == len(blocks) - 1:
            ready = len(blocks)

        @pl.when(has_outer)
        def _():
            for earlier in range(done, ready):
                finish(earlier, True)

        done = ready

    @pl.when(jnp.logical_not(has_outer))
    def _():
        for number in range(len(blocks)):
            finish(number, False)

    edges_out.wait()
    for copy in [whole_in, whole_out, to_next, to_prev, back_prev, back_next] + x_copies + y_copies + fx_copies + fy_copies:
        copy.wait_send()
    for number in range(len(blocks)):
        core_copies[0, number].wait_send()
        core_copies[1, number].wait_send()
        x_grad_copies[number].wait_send()
        inward(number, True).wait_send()

    @pl.when(has_outer)
    def _():
        for number in range(len(blocks)):
            outward(number).wait_send()


emit_pieces = 4


def emit(*refs):
    copies = []
    for number in range(4):
        source, target = refs[number], refs[4 + number]
        size = source.shape[0] // emit_pieces
        if size % 8:
            spans = [pl.ds(0, source.shape[0])]
        else:
            spans = [pl.ds(start, size) for start in range(0, source.shape[0], size)]
        for place, span in enumerate(spans):
            copies.append(
                (
                    pltpu.make_async_copy(source.at[span], refs[8 + number].at[span], refs[12].at[number, place]),
                    pltpu.make_async_copy(refs[8 + number].at[span], target.at[span], refs[13].at[number, place]),
                )
            )
    for load, _ in copies:
        load.start()
    for load, store in copies:
        load.wait()
        store.start()
    for _, store in copies:
        store.wait()


def body(mesh_shape, nodes, edges, senders, receivers, halo_rows, drop_mask, w_in, w_out, cotangent):
    count_nodes, depth = nodes.shape
    count_edges = edges.shape[0]
    halo_size = halo_rows.shape[0] // 2
    padded = -(-halo_size // 16) * 16
    doms = mesh_shape["dom"]
    sizes = {
        "groups": mesh_shape["groups"],
        "dom": doms,
        "gather_in": (3, 3, 3, 2, 1),
        "gather_out": (1, 1),
        "lag": 64,
        "sum_out": (1, 1, 1, 1),
        "sum_in": (4, 4, 4, 4, 4, 4, 4, 4, 4, 4, 2, 2, 2, 1, 1),
        "halo": halo_size,
        "factor": 1.0 / math.sqrt(count_edges * doms * mesh_shape["mp"]),
    }
    vmem = pl.BlockSpec(memory_space=pltpu.VMEM)
    pieces = len(sizes["gather_in"]) + len(sizes["gather_out"])
    count = len(sizes["sum_in"]) + len(sizes["sum_out"])
    piece = (w_in.shape[0] + w_out.shape[0], depth)
    hbm = pl.BlockSpec(memory_space=pl.ANY)
    dma = pltpu.SemaphoreType.DMA
    results = pl.pallas_call(
        functools.partial(kernel, sizes),
        out_shape=(
            jax.ShapeDtypeStruct(nodes.shape, f32),
            jax.ShapeDtypeStruct(edges.shape, f32),
            jax.ShapeDtypeStruct(w_in.shape, f32),
            jax.ShapeDtypeStruct(w_out.shape, f32),
        ),
        in_specs=[vmem, hbm, vmem, vmem, vmem, vmem, hbm, hbm, hbm],
        out_specs=(vmem, hbm, vmem, vmem),
        scratch_shapes=[
            pltpu.VMEM((2 * count_nodes + 2 * padded, depth), f32),
            pltpu.VMEM((3 * depth, depth), f32),
            pltpu.VMEM((depth, depth), f32),
            pltpu.VMEM((2, padded, depth), f32),
            pltpu.VMEM((2, padded, depth), f32),
            pltpu.VMEM((2 * padded, depth), f32),
            pltpu.VMEM((3 * depth, depth), f32),
            pltpu.VMEM((depth, depth), f32),
            pltpu.VMEM((2,) + piece, f32),
            pltpu.VMEM(piece, f32),
            pltpu.VMEM(piece, f32),
            pltpu.VMEM(piece, f32),
            pltpu.VMEM(piece, f32),
            pltpu.VMEM(piece, f32),
            pltpu.VMEM(piece, f32),
            dma((5, pieces)),
            dma((5, pieces)),
            dma((4,)),
            dma((4,)),
            dma((2, count)),
            dma((2, count)),
            dma((count,)),
            dma((count,)),
            dma((count,)),
            dma((count,)),
            dma((count,)),
            dma((count,)),
            pltpu.VMEM(edges.shape, f32),
            pltpu.VMEM(edges.shape, f32),
            pltpu.VMEM(edges.shape, f32),
            pltpu.VMEM(nodes.shape, f32),
            dma((5,)),
        ],
        compiler_params=pltpu.CompilerParams(
            collective_id=0, has_side_effects=True, vmem_limit_bytes=56 * 1024 * 1024
        ),
    )(
        nodes, edges, senders, receivers, halo_rows, drop_mask, w_in, w_out, cotangent
    )
    return pl.pallas_call(
        emit,
        out_shape=tuple(jax.ShapeDtypeStruct(result.shape, f32) for result in results),
        in_specs=[hbm] * 4,
        out_specs=(hbm,) * 4,
        scratch_shapes=[pltpu.VMEM(result.shape, f32) for result in results] + [dma((4, emit_pieces))] * 2,
    )(*results)


def solution(mesh):
    return jax.shard_map(
        functools.partial(body, dict(mesh.shape)),
        mesh=mesh,
        in_specs=(
            P(("groups", "dom", "mp"), None),
            P(("groups", "dom", "mp"), None),
            P(("dom", "mp")),
            P(("dom", "mp")),
            P(("dom", "mp")),
            P(("dom", "mp")),
            P("mp", None),
            P("mp", None),
            P(("groups", "dom", "mp"), None),
        ),
        out_specs=(
            P(("groups", "dom", "mp"), None),
            P(("groups", "dom", "mp"), None),
            P(("groups", "mp"), None),
            P(("groups", "mp"), None),
        ),
        check_vma=False,
    )
```
